32 devices in a mesh: groups: 2 (over y), space: 4 (over z), hidden: 2 (over x), sub: 2 (over core).
Axes of the slice: x: 2, y: 2, z: 4, core: 2. Of those that a mesh axis runs over, the one named last changes fastest.
Arguments:
- agent_state: bfloat16 [8192, 256], P(('groups', 'space')), parts along dimension 0, may hold values from -6 to 6
- members: int32 [8, 1024], P(('groups', 'space')), parts along dimension 0, may hold values from 0 to 1023, each once within a row
- norm_gain: float32 [256], replicated, may hold values from 0.1 to 1.9
- w_recv: bfloat16 [256, 1024], P(None, 'hidden'), may hold values from -0.375 to 0.375
- w_send: bfloat16 [256, 1024], P(None, 'hidden'), may hold values from -1.5 to 1.5
- w_out: bfloat16 [1024, 256], P('hidden'), may hold values from -0.1875 to 0.1875
- pair_list: int32 [512, 2], P(('groups', 'space', 'sub')), parts along dimension 0, may hold values from 0 to 31, as said below
- pair_counts: int32 [16], P(('groups', 'space', 'sub')), parts along dimension 0, may hold values from 0 to 32, as said below
- cotangent: bfloat16 [8192, 256], P(('groups', 'space')), parts along dimension 0, may hold values from -6 to 6
Outputs:
- new_state: bfloat16 [8192, 256], P(('groups', 'space', 'hidden', 'sub')), parts along dimension 0
- grad_state: float32 [8192, 256], P(('groups', 'space', 'hidden', 'sub')), parts along dimension 0
- grad_recv: float32 [512, 1024], P('groups', 'hidden'), parts along dimension 0
- grad_send: float32 [512, 1024], P('groups', 'hidden'), parts along dimension 0
- grad_out: float32 [2048, 256], P(('groups', 'hidden')), parts along dimension 0
The draws below stay inside these ranges and needn't reach their ends.
There are 2 independent parts, one for each index of `groups`. The reference program is written for one: setup_inputs(seed, part) draws one part's arguments, and reference() takes and returns one part's arrays. A program takes and returns all parts, laid end to end along the dimension named above; an argument that names none is the same for every part. Nothing has to cross between parts.
Inputs may be any that keep to these rules, and one draw needn't show every extreme that they name: `pair_list`: rows p * 32 to p * 32 + pair_counts[p] - 1 hold the pairs of owning device p = 2 * (space index) + (sub index); each is (s, t) with s a block of that device's region and s < t <= s + 8; no pair appears twice in a part; other rows are 0. `pair_counts`: some device holds exactly 32 live pairs. `members`: each row is a permutation.
All inputs are finite; a program needn't handle non-finite values.
Results may differ from the reference program's by a relative error of at most 0.0095.
Values may be sent and summed in bfloat16 or wider, within the bound.
A program may use at most 64 MiB of HBM per device.

```python
import math
import jax
import jax.numpy as jnp
from jax import lax

D = 256
HID = 1024
BLK = 128
BLK_DEV = 8
PAIR_DEV = 32
AG_DEV = 1024
REGIONS = 4
AGENTS = 4096
BLOCKS = 32
PAIRS = 256
N_SPACE = 4


def region_lists(key):
    cand_count = BLK_DEV * BLK_DEV

    def one_region(region):
        region_key = jax.random.fold_in(key, region)
        order_key, total_key, split_key = jax.random.split(region_key, 3)
        cand_ids = jnp.arange(cand_count, dtype=jnp.int32)
        sources = region * BLK_DEV + cand_ids // BLK_DEV
        targets = sources + cand_ids % BLK_DEV + 1
        valid = (targets < BLK_DEV * N_SPACE).astype(jnp.int32)
        scores = valid * cand_count + jax.random.permutation(order_key, cand_count).astype(jnp.int32)
        picked = jnp.argsort(-scores, stable=True)
        total = jnp.minimum(jax.random.randint(total_key, (), 1, PAIR_DEV + 1), jnp.sum(valid))
        first = jax.random.randint(split_key, (), 0, total + 1)
        return (sources[picked], targets[picked], total, first)
    regions_all = jnp.arange(N_SPACE, dtype=jnp.int32)
    sources, targets, totals, firsts = jax.vmap(one_region)(regions_all)
    dense_key, extra_key, coin_key = jax.random.split(jax.random.fold_in(key, 977), 3)
    dense_region = jax.random.randint(dense_key, (), 0, N_SPACE - 1)
    dense_total = PAIR_DEV + jax.random.randint(extra_key, (), 0, PAIR_DEV // 2 + 1)
    coin_flip = jax.random.randint(coin_key, (), 0, 2)
    dense_first = jnp.where(coin_flip == 0, PAIR_DEV, dense_total - PAIR_DEV)
    is_dense = regions_all == dense_region
    totals = jnp.where(is_dense, dense_total, totals)
    firsts = jnp.where(is_dense, dense_first, firsts)
    slot_ids = jnp.arange(PAIR_DEV, dtype=jnp.int32)
    count_zero = firsts
    count_one = totals - firsts
    index_zero = jnp.minimum(slot_ids[None, :], cand_count - 1)
    index_one = jnp.minimum(firsts[:, None] + slot_ids[None, :], cand_count - 1)
    live_zero = slot_ids[None, :] < count_zero[:, None]
    live_one = slot_ids[None, :] < count_one[:, None]
    src_zero = jnp.where(live_zero, jnp.take_along_axis(sources, index_zero, 1), 0)
    tgt_zero = jnp.where(live_zero, jnp.take_along_axis(targets, index_zero, 1), 0)
    src_one = jnp.where(live_one, jnp.take_along_axis(sources, index_one, 1), 0)
    tgt_one = jnp.where(live_one, jnp.take_along_axis(targets, index_one, 1), 0)
    lists_zero = jnp.stack([src_zero, tgt_zero], axis=-1)
    lists_one = jnp.stack([src_one, tgt_one], axis=-1)
    pair_rows = jnp.stack([lists_zero, lists_one], axis=1).reshape(-1, 2).astype(jnp.int32)
    counts_all = jnp.stack([count_zero, count_one], axis=1).reshape(-1).astype(jnp.int32)
    return (pair_rows, counts_all)


def draw_pair_list(key, part):
    pair_rows, counts_all = region_lists(key)
    return pair_rows


def draw_pair_counts(key, part):
    pair_rows, counts_all = region_lists(key)
    return counts_all


def levels(own_key, dims, pieces, smallest, largest):
    def one(position, parts):
        heights = jax.random.uniform(jax.random.fold_in(jax.random.fold_in(own_key, 6), position), (parts,), jnp.float32, smallest / len(pieces), largest / len(pieces))
        return jnp.repeat(jnp.exp(heights), dims[position] // parts).reshape((-1,) + (1,) * (len(dims) - position - 1))

    loudness = one(*pieces[0])
    for cut in pieces[1:]:
        loudness = loudness * one(*cut)
    return loudness


def scatter_about(own_key, extent, spread, most, pieces=(), held_as=jnp.bfloat16):
    values = spread * jax.random.normal(own_key, extent, jnp.float32)
    if pieces:
        values = values * levels(own_key, extent, pieces, -0.22, 0.18)
    return jnp.clip(values, -most, most).astype(held_as)


def setup_inputs(seed: int = 0, part: int = 0) -> dict:
    arg_keys = jax.random.split(jax.random.key(seed), 10)
    part_keys = jax.random.split(jax.random.fold_in(arg_keys[9], part), 10)
    agent_state = scatter_about(part_keys[0], (AGENTS, D), 1.0, 6.0, ((0, 4),))
    members = jax.vmap(lambda own: jax.random.permutation(own, AG_DEV))(jax.random.split(part_keys[1], REGIONS)).reshape((REGIONS, AG_DEV)).astype(jnp.int32)
    norm_gain = jnp.clip(1.0 + 0.18 * jax.random.normal(arg_keys[2], (D,), jnp.float32), 0.1, 1.9)
    w_recv = scatter_about(arg_keys[3], (D, HID), D ** -0.5, 0.375, ((1, 2),))
    w_send = scatter_about(arg_keys[4], (D, HID), (D // 16) ** -0.5, 1.5, ((1, 2),))
    w_out = scatter_about(arg_keys[5], (HID, D), HID ** -0.5, 0.1875, ((0, 2),))
    pair_list = draw_pair_list(jax.random.fold_in(jax.random.fold_in(arg_keys[9], part), 71), part)
    pair_counts = draw_pair_counts(jax.random.fold_in(jax.random.fold_in(arg_keys[9], part), 71), part)
    cotangent = scatter_about(part_keys[8], (AGENTS, D), 1.0, 6.0, ((0, 4),))
    return {"agent_state": agent_state, "members": members, "norm_gain": norm_gain, "w_recv": w_recv, "w_send": w_send, "w_out": w_out, "pair_list": pair_list, "pair_counts": pair_counts, "cotangent": cotangent}


GELU_K = math.sqrt(2.0 / math.pi)

def gelu_tanh(pre_act):
    return 0.5 * pre_act * (1.0 + jnp.tanh(GELU_K * (pre_act + 0.044715 * pre_act * pre_act * pre_act)))

def gelu_slope(pre_act):
    tanh_part = jnp.tanh(GELU_K * (pre_act + 0.044715 * pre_act * pre_act * pre_act))
    inner = GELU_K * (1.0 + 3.0 * 0.044715 * pre_act * pre_act)
    return 0.5 * (1.0 + tanh_part) + 0.5 * pre_act * (1.0 - tanh_part * tanh_part) * inner

def normalize(state_rows, norm_gain):
    factor = lax.rsqrt(lax.optimization_barrier(jnp.mean(state_rows * state_rows, axis=-1, keepdims=True)) + 1e-06)
    return state_rows * factor * norm_gain

def norm_backward(state_rows, norm_gain, upstream):
    factor = lax.rsqrt(lax.optimization_barrier(jnp.mean(state_rows * state_rows, axis=-1, keepdims=True)) + 1e-06)
    scaled = upstream * norm_gain
    inner = lax.optimization_barrier(jnp.mean(state_rows * scaled, axis=-1, keepdims=True))
    return factor * scaled - state_rows * factor * factor * factor * inner

def block_means(normed):
    width = normed.shape[1]
    summed = lax.optimization_barrier(jnp.sum(normed.astype(jnp.float32).reshape(-1, BLK, width), axis=1))
    return (summed / BLK).astype(jnp.bfloat16)

def spread_blocks(values):
    count = values.shape[0]
    width = values.shape[1]
    return jnp.broadcast_to((values / BLK)[:, None, :], (count, BLK, width)).reshape(count * BLK, width)

def add_rows(total, start, value):
    current = lax.dynamic_slice_in_dim(total, start, value.shape[0], 0)
    return lax.dynamic_update_slice_in_dim(total, current + value, start, 0)

def one_side(recv_rows, send_vec, grad_rows, w_recv, w_out):
    pre_act = jnp.dot(recv_rows, w_recv, preferred_element_type=jnp.float32) + send_vec[None, :]
    act_rows = gelu_tanh(pre_act).astype(jnp.bfloat16)
    message = jnp.dot(act_rows, w_out, preferred_element_type=jnp.float32)
    d_act = jnp.dot(grad_rows, w_out.T, preferred_element_type=jnp.float32)
    d_pre = (d_act * gelu_slope(pre_act)).astype(jnp.bfloat16)
    grad_out = jnp.dot(act_rows.T, grad_rows, preferred_element_type=jnp.float32)
    grad_recv = jnp.dot(recv_rows.T, d_pre, preferred_element_type=jnp.float32)
    grad_in = jnp.dot(d_pre, w_recv.T, preferred_element_type=jnp.float32)
    grad_vec = lax.optimization_barrier(jnp.sum(d_pre.astype(jnp.float32), axis=0))
    return (message, grad_in, grad_vec, grad_recv, grad_out)

def pair_update(carry, source, target, live_scale, normed, grad_src, send_proj, w_recv, w_out):
    messages, row_grads, proj_grads, grad_recv, grad_out = carry
    for receiver, sender in ((target, source), (source, target)):
        start = (receiver * BLK).astype(jnp.int32)
        recv_rows = lax.dynamic_slice_in_dim(normed, start, BLK, 0)
        grad_rows = lax.dynamic_slice_in_dim(grad_src, start, BLK, 0)
        send_vec = lax.dynamic_index_in_dim(send_proj, sender.astype(jnp.int32), 0, keepdims=False)
        message, grad_in, grad_vec, part_recv, part_out = one_side(recv_rows, send_vec, grad_rows, w_recv, w_out)
        messages = add_rows(messages, start, live_scale * message)
        row_grads = add_rows(row_grads, start, live_scale * grad_in)
        proj_grads = add_rows(proj_grads, sender.astype(jnp.int32), live_scale * grad_vec[None, :])
        grad_recv = grad_recv + live_scale * part_recv
        grad_out = grad_out + live_scale * part_out
    return (messages, row_grads, proj_grads, grad_recv, grad_out)

def reference(agent_state, members, norm_gain, w_recv, w_send, w_out, pair_list, pair_counts, cotangent):
    offsets = jnp.arange(N_SPACE, dtype=jnp.int32)[:, None] * AG_DEV
    slot_order = (offsets + members.astype(jnp.int32)).reshape(-1)
    state_slots = agent_state.astype(jnp.float32)[slot_order]
    normed = normalize(state_slots, norm_gain).astype(jnp.bfloat16)
    summary = block_means(normed)
    send_proj = jnp.dot(summary, w_send, preferred_element_type=jnp.float32)
    slot_ids = jnp.arange(PAIRS, dtype=jnp.int32)
    live = (slot_ids % PAIR_DEV < pair_counts[slot_ids // PAIR_DEV]).astype(jnp.float32)
    initial = (jnp.zeros((AGENTS, D), jnp.float32), jnp.zeros((AGENTS, D), jnp.float32), jnp.zeros((BLOCKS, HID), jnp.float32), jnp.zeros((D, HID), jnp.float32), jnp.zeros((HID, D), jnp.float32))

    def visit(carry, inputs):
        pair_row, live_scale = inputs
        carry = pair_update(carry, pair_row[0], pair_row[1], live_scale, normed, cotangent, send_proj, w_recv, w_out)
        return (carry, None)
    carry, unused = lax.scan(visit, initial, (pair_list, live))
    messages, row_grads, proj_grads, grad_recv, grad_out = carry
    grad_send = jnp.dot(summary.astype(jnp.float32).T, proj_grads, precision=lax.Precision.HIGHEST)
    summary_grads = jnp.dot(proj_grads, w_send.astype(jnp.float32).T, precision=lax.Precision.HIGHEST)
    row_grads = row_grads + spread_blocks(summary_grads)
    new_state = (state_slots + messages).astype(jnp.bfloat16)
    grad_state = norm_backward(state_slots, norm_gain, row_grads) + cotangent.astype(jnp.float32)
    return (new_state, grad_state, grad_recv, grad_send, grad_out)
```

```python
import functools
import math

import jax
import jax.numpy as jnp
from jax import lax
from jax.experimental import pallas as pl
from jax.experimental.pallas import tpu as pltpu
from jax.sharding import PartitionSpec as P

BLK = 128
CHUNK = 16
BF16 = jnp.bfloat16
F32 = jnp.float32
MESH = pl.DeviceIdType.MESH
HIGH = lax.Precision.HIGHEST

GELU_K = math.sqrt(2.0 / math.pi)
BETA = (GELU_K * 0.044715) ** (1.0 / 3.0)
KAPPA = GELU_K / BETA


def dot(a, b, dims=((1,), (0,)), precision=None):
    return lax.dot_general(
        a, b, (dims, ((), ())), preferred_element_type=F32, precision=precision
    )


def kernel(
    dims,
    state_ref,
    memb_ref,
    gain_ref,
    wr_ref,
    ws_ref,
    wo_ref,
    pairs_ref,
    counts_ref,
    cot_ref,
    new_ref,
    gst_ref,
    gr_ref,
    gs_ref,
    go_ref,
    x_buf,
    xs_buf,
    lists,
    win,
    proj,
    mask,
    pre_buf,
    dact_buf,
    a_buf,
    d_buf,
    pg_buf,
    msg_send,
    msg_recv,
    own_msg,
    sg_loc,
    sg_near,
    sg_reg,
    sg_peer,
    w_loc,
    w_send,
    w_recv,
    w_all,
    list_ss,
    list_rs,
    win_ss,
    win_rs,
    msg_ss,
    msg_rs,
    near_ss,
    near_rs,
    peer_ss,
    peer_rs,
    red_ss,
    red_rs,
    gat_ss,
    gat_rs,
    fwd_ss,
    fwd_rs,
):
    nz, nh, ns = dims
    rows, width = state_ref.shape
    blocks = rows // BLK
    slots = pairs_ref.shape[0]
    quarter = wr_ref.shape[1] // ns
    owners = nh * ns
    own_blocks = blocks // owners
    piece = own_blocks * BLK
    r = lax.axis_index("space")
    h = lax.axis_index("hidden")
    s = lax.axis_index("sub")
    after = lax.rem(r + 1, nz)
    before = lax.rem(r + nz - 1, nz)

    def peer(dh, ds):
        return lax.rem(h + dh, nh), lax.rem(s + ds, ns)

    offsets = [(dh, ds) for dh in range(nh - 1, -1, -1) for ds in range(ns - 1, -1, -1)]

    barrier = pltpu.get_barrier_semaphore()
    met = 0
    for k in range(1, nz):
        pl.semaphore_signal(
            barrier, inc=1, device_id={"space": lax.rem(r + k, nz)}, device_id_type=MESH
        )
        met += 1
    for dh, ds in offsets[:-1]:
        ph, ps = peer(dh, ds)
        pl.semaphore_signal(
            barrier, inc=1, device_id={"hidden": ph, "sub": ps}, device_id_type=MESH
        )
        met += 1
    for ds in range(1, ns):
        for other in (after, before):
            pl.semaphore_signal(
                barrier,
                inc=1,
                device_id={"space": other, "sub": lax.rem(s + ds, ns)},
                device_id_type=MESH,
            )
            met += 1

    live = lax.broadcasted_iota(jnp.int32, (slots, 128), 0) < counts_ref[0]
    for column in range(2):
        ids = jnp.broadcast_to(pairs_ref[:, column : column + 1], (slots, 128))
        lists[0, column * slots : (column + 1) * slots, :] = jnp.where(live, ids, -1000000)

    gain = gain_ref[...]
    for k in range(rows // 256):
        hot = lax.broadcasted_iota(jnp.int32, (rows, 256), 0) == memb_ref[:, k * 256 : (k + 1) * 256]
        xs = dot(hot.astype(F32).astype(BF16), state_ref[...], ((0,), (0,)))
        factor = lax.rsqrt(jnp.mean(xs * xs, axis=-1, keepdims=True) + 1e-06)
        normed = (xs * factor * gain).astype(BF16)
        x_buf[k * 256 : (k + 1) * 256, :] = normed
        xs_buf[k * 256 : (k + 1) * 256, :] = xs.astype(BF16)
        means = jnp.sum(normed.astype(F32).reshape(256 // BLK, BLK, width), axis=1) / BLK
        first = blocks + k * (256 // BLK)
        win[first : first + 256 // BLK, :] = means.astype(BF16).astype(F32)

    pl.semaphore_wait(barrier, met)

    copies = []

    def send(src, dst, ss, rs, where):
        copy = pltpu.make_async_remote_copy(
            src_ref=src,
            dst_ref=dst,
            send_sem=ss,
            recv_sem=rs,
            device_id=where,
            device_id_type=MESH,
        )
        copy.start()
        return copy

    for n, (other, place) in enumerate(((before, 2 * blocks), (after, 0))):
        copies.append(
            send(
                win.at[pl.ds(blocks, blocks)],
                win.at[pl.ds(place, blocks)],
                win_ss.at[n],
                win_rs.at[n],
                {"space": other},
            )
        )
    for ds in range(1, ns):
        copies.append(
            send(
                lists.at[0],
                lists.at[ds],
                list_ss.at[ds - 1],
                list_rs.at[ds - 1],
                {"sub": lax.rem(s + ds, ns)},
            )
        )
    for ds in range(ns):
        copies.append(
            send(
                lists.at[0],
                lists.at[ns + ds],
                list_ss.at[ns - 1 + ds],
                list_rs.at[ns - 1 + ds],
                {"space": after, "sub": lax.rem(s + ds, ns)},
            )
        )

    own_cols = pl.ds(pl.multiple_of(s * quarter, quarter), quarter)
    wr = wr_ref[:, own_cols]
    wo = wo_ref[own_cols, :]
    ws = ws_ref[:, own_cols]
    for k in range(rows // 256):
        part = slice(k * 256, (k + 1) * 256)
        pre_buf[part, :] = dot(x_buf[part, :], wr) * BETA
        dact_buf[part, :] = dot(cot_ref[part, :], wo, ((1,), (1,)))
    pg_buf[...] = jnp.zeros_like(pg_buf)

    for copy in copies:
        copy.wait()

    span = 4 * blocks
    base = r * blocks
    marks = []
    lane = lax.broadcasted_iota(jnp.int32, (slots, 128), 1)
    for n in range(2 * ns):
        source = lists[n, 0:slots, :] - base
        target = lists[n, slots : 2 * slots, :] - base
        for recv, sender in ((target, source), (source, target)):
            inside = (recv >= 0) & (recv < blocks)
            place = jnp.where(inside, recv * span + (sender - recv + blocks), -1)
            marks.append(
                jnp.concatenate(
                    [
                        (place == lane + c * 128).astype(F32).astype(BF16)
                        for c in range(blocks * span // 128)
                    ],
                    axis=1,
                )
            )
    marks = jnp.concatenate(marks, axis=0)
    mask[...] = dot(marks, jnp.ones((marks.shape[0], quarter), BF16), ((0,), (0,)))
    proj[...] = dot(win[...].astype(BF16), ws) * BETA

    def one_block(a):
        def one_chunk(c, carry):
            here = pl.ds(pl.multiple_of(a * BLK + c * CHUNK, CHUNK), CHUNK)
            v0 = pre_buf[here, :]
            da = dact_buf[here, :]
            act_sum = jnp.zeros((CHUNK, quarter), F32)
            d_sum = jnp.zeros((CHUNK, quarter), F32)
            for d in range(2 * blocks + 1):
                if d == blocks:
                    continue
                v = v0 + proj[pl.ds(a + d, 1), :]
                v2 = v * v
                t = jnp.tanh(v * (v2 + KAPPA))
                rise = (1.0 + t) * mask[pl.ds(a * span + d, 1), :]
                act = v * rise
                act_sum = act_sum + act
                slope = rise + act * (1.0 - t) * (3.0 * v2 + KAPPA)
                d_pre = da * slope
                d_sum = d_sum + d_pre
                pg = pl.ds(pl.multiple_of((a + d) * 8, 8), 8)
                total = d_pre[0:8, :]
                for i in range(1, CHUNK // 8):
                    total = total + d_pre[i * 8 : (i + 1) * 8, :]
                pg_buf[pg, :] = pg_buf[pg, :] + total
            a_buf[here, :] = (act_sum * (0.5 / BETA)).astype(BF16)
            d_buf[here, :] = (d_sum * 0.5).astype(BF16)
            return carry

        lax.fori_loop(0, BLK // CHUNK, one_chunk, 0)

    msg_copies = []
    for n, (dh, ds) in enumerate(offsets):
        ph, ps = peer(dh, ds)
        first = (ph * ns + ps) * own_blocks

        def step(i, carry, first=first):
            one_block(first + i)
            return carry

        lax.fori_loop(0, own_blocks, step, 0)
        here = pl.ds(pl.multiple_of(first * BLK, BLK), piece)
        message = dot(a_buf[here, :], wo)
        grads = dot(d_buf[here, :], wr, ((1,), (1,)))
        if n < owners - 1:
            msg_send[n, 0:piece, :] = message.astype(BF16)
            msg_send[n, piece : 2 * piece, :] = grads.astype(BF16)
            msg_copies.append(
                send(
                    msg_send.at[n],
                    msg_recv.at[n],
                    msg_ss.at[n],
                    msg_rs.at[n],
                    {"hidden": ph, "sub": ps},
                )
            )
        else:
            own_msg[0:piece, :] = message
            own_msg[piece : 2 * piece, :] = grads

    pg = jnp.sum(pg_buf[...].reshape(3 * blocks, 8, quarter), axis=1) * 0.5
    sg_loc[...] = dot(pg, ws.astype(F32), ((1,), (1,)), HIGH)
    near = [
        send(
            sg_loc.at[pl.ds(place, blocks)],
            sg_near.at[n],
            near_ss.at[n],
            near_rs.at[n],
            {"space": other},
        )
        for n, (other, place) in enumerate(((before, 0), (after, 2 * blocks)))
    ]

    w_loc[0:width, :] = dot(x_buf[...], d_buf[...], ((0,), (0,)))
    w_loc[width : 2 * width, :] = dot(win[...], pg, ((0,), (0,)), HIGH)
    for c in range(width // quarter):
        w_loc[2 * width + c * quarter : 2 * width + (c + 1) * quarter, :] = dot(
            a_buf[...], cot_ref[:, c * quarter : (c + 1) * quarter], ((0,), (0,))
        )
    travel = w_send.dtype
    w_send[...] = w_loc[...].astype(travel)
    share = 3 * width // nz

    def share_at(index):
        return pl.ds(pl.multiple_of(index * share, share), share)

    reduces = []
    for k in range(1, nz):
        to = lax.rem(r + k, nz)
        reduces.append(
            send(
                w_send.at[share_at(to)],
                w_recv.at[k - 1],
                red_ss.at[k - 1],
                red_rs.at[k - 1],
                {"space": to},
            )
        )

    for copy in near:
        copy.wait()
    sg_reg[...] = sg_loc[blocks : 2 * blocks, :] + sg_near[0] + sg_near[1]
    peers = []
    for n, (dh, ds) in enumerate(offsets[:-1]):
        ph, ps = peer(dh, ds)
        peers.append(
            send(
                sg_reg,
                sg_peer.at[n],
                peer_ss.at[n],
                peer_rs.at[n],
                {"hidden": ph, "sub": ps},
            )
        )

    for copy in reduces:
        copy.wait_recv()
    total = w_loc[share_at(r), :]
    for k in range(1, nz):
        total = total + w_recv[k - 1].astype(F32)
    w_all[0, share_at(r), :] = total.astype(travel)
    gathers = []
    forwards = []
    for k in range(1, nz):
        gathers.append(
            send(
                w_all.at[0, share_at(r)],
                w_all.at[0, share_at(r)],
                gat_ss.at[k - 1],
                gat_rs.at[k - 1],
                {"space": lax.rem(r + k, nz)},
            )
        )

    def forward(k):
        origin = share_at(lax.rem(r + nz - k, nz))
        for ds in range(1, ns):
            forwards.append(
                send(
                    w_all.at[0, origin],
                    w_all.at[ds, origin],
                    fwd_ss.at[ds - 1, k],
                    fwd_rs.at[ds - 1, k],
                    {"sub": lax.rem(s + ds, ns)},
                )
            )

    forward(0)

    for copy in msg_copies:
        copy.wait()
    for copy in peers:
        copy.wait()
    message = own_msg[0:piece, :]
    grads = own_msg[piece : 2 * piece, :]
    near_sum = sg_reg[...]
    for n in range(owners - 1):
        message = message + msg_recv[n, 0:piece, :].astype(F32)
        grads = grads + msg_recv[n, piece : 2 * piece, :].astype(F32)
        near_sum = near_sum + sg_peer[n]
    sg_loc[0:blocks, :] = near_sum / BLK
    q = h * ns + s
    mine = pl.ds(pl.multiple_of(q * piece, piece), piece)
    xs = xs_buf[mine, :].astype(F32)
    new_ref[...] = (xs + message).astype(BF16)
    spread = jnp.concatenate(
        [
            jnp.broadcast_to(sg_loc[pl.ds(q * own_blocks + i, 1), :], (BLK, width))
            for i in range(own_blocks)
        ],
        axis=0,
    )
    factor = lax.rsqrt(jnp.mean(xs * xs, axis=-1, keepdims=True) + 1e-06)
    scaled = (grads + spread) * gain
    inner = jnp.mean(xs * scaled, axis=-1, keepdims=True)
    gst_ref[...] = (
        factor * scaled - xs * factor * factor * factor * inner + cot_ref[mine, :].astype(F32)
    )

    for k in range(1, nz):
        gathers[k - 1].wait_recv()
        forward(k)
    for copy in forwards:
        copy.wait_recv()
    for ds in range(ns):
        begin = pl.multiple_of(lax.rem(s + ns - ds, ns) * quarter, quarter)
        cols = pl.ds(begin, quarter)
        gr_ref[:, cols] = w_all[ds, 0:width, :].astype(F32)
        gs_ref[:, cols] = w_all[ds, width : 2 * width, :].astype(F32)
        for c in range(width // quarter):
            at = 2 * width + c * quarter
            go_ref[cols, c * quarter : (c + 1) * quarter] = w_all[ds, at : at + quarter, :].astype(
                F32
            )
    for copy in reduces + gathers + forwards:
        copy.wait_send()


def on_device(
    dims,
    agent_state,
    members,
    norm_gain,
    w_recv,
    w_send,
    w_out,
    pair_list,
    pair_counts,
    cotangent,
):
    nz, nh, ns = dims
    rows, width = agent_state.shape
    blocks = rows // BLK
    slots = pair_list.shape[0]
    hid_dev = w_recv.shape[1]
    quarter = hid_dev // ns
    owners = nh * ns
    piece = rows // owners
    share = 3 * width // nz
    travel = BF16 if share % 16 == 0 else F32
    dma = pltpu.SemaphoreType.DMA
    vmem = pl.BlockSpec(memory_space=pltpu.VMEM)
    smem = pl.BlockSpec(memory_space=pltpu.SMEM)
    return pl.pallas_call(
        functools.partial(kernel, dims),
        out_shape=(
            jax.ShapeDtypeStruct((piece, width), BF16),
            jax.ShapeDtypeStruct((piece, width), F32),
            jax.ShapeDtypeStruct((width, hid_dev), F32),
            jax.ShapeDtypeStruct((width, hid_dev), F32),
            jax.ShapeDtypeStruct((hid_dev, width), F32),
        ),
        in_specs=[vmem] * 7 + [smem, vmem],
        out_specs=(vmem,) * 5,
        scratch_shapes=[
            pltpu.VMEM((rows, width), BF16),
            pltpu.VMEM((rows, width), BF16),
            pltpu.VMEM((2 * ns, 2 * slots, 128), jnp.int32),
            pltpu.VMEM((3 * blocks, width), F32),
            pltpu.VMEM((3 * blocks, quarter), F32),
            pltpu.VMEM((4 * blocks * blocks, quarter), F32),
            pltpu.VMEM((rows, quarter), F32),
            pltpu.VMEM((rows, quarter), F32),
            pltpu.VMEM((rows, quarter), BF16),
            pltpu.VMEM((rows, quarter), BF16),
            pltpu.VMEM((3 * blocks * 8, quarter), F32),
            pltpu.VMEM((owners - 1, 2 * piece, width), BF16),
            pltpu.VMEM((owners - 1, 2 * piece, width), BF16),
            pltpu.VMEM((2 * piece, width), F32),
            pltpu.VMEM((3 * blocks, width), F32),
            pltpu.VMEM((2, blocks, width), F32),
            pltpu.VMEM((blocks, width), F32),
            pltpu.VMEM((owners - 1, blocks, width), F32),
            pltpu.VMEM((3 * width, quarter), F32),
            pltpu.VMEM((3 * width, quarter), travel),
            pltpu.VMEM((nz - 1, share, quarter), travel),
            pltpu.VMEM((ns, 3 * width, quarter), travel),
            dma((2 * ns - 1,)),
            dma((2 * ns - 1,)),
            dma((2,)),
            dma((2,)),
            dma((owners - 1,)),
            dma((owners - 1,)),
            dma((2,)),
            dma((2,)),
            dma((owners - 1,)),
            dma((owners - 1,)),
            dma((nz - 1,)),
            dma((nz - 1,)),
            dma((nz - 1,)),
            dma((nz - 1,)),
            dma((ns - 1, nz)),
            dma((ns - 1, nz)),
        ],
        compiler_params=pltpu.CompilerParams(
            collective_id=0, has_side_effects=True, vmem_limit_bytes=48 * 1024 * 1024
        ),
    )(
        agent_state,
        members,
        norm_gain.reshape(1, width),
        w_recv,
        w_send,
        w_out,
        pair_list,
        pair_counts,
        cotangent,
    )


def solution(mesh):
    in_specs = (
        P(("groups", "space"), None),
        P(("groups", "space"), None),
        P(),
        P(None, "hidden"),
        P(None, "hidden"),
        P("hidden", None),
        P(("groups", "space", "sub"), None),
        P(("groups", "space", "sub")),
        P(("groups", "space"), None),
    )
    out_specs = (
        P(("groups", "space", "hidden", "sub"), None),
        P(("groups", "space", "hidden", "sub"), None),
        P("groups", "hidden"),
        P("groups", "hidden"),
        P(("groups", "hidden"), None),
    )
    dims = (mesh.shape["space"], mesh.shape["hidden"], mesh.shape["sub"])
    return jax.shard_map(
        functools.partial(on_device, dims),
        mesh=mesh,
        in_specs=in_specs,
        out_specs=out_specs,
        check_vma=False,
    )
```

```python
import functools
import math

import jax
import jax.numpy as jnp
from jax import lax
from jax.experimental import pallas as pl
from jax.experimental.pallas import tpu as pltpu
from jax.sharding import PartitionSpec as P

BLK = 128
CHUNK = 16
BF16 = jnp.bfloat16
F32 = jnp.float32
MESH = pl.DeviceIdType.MESH
HIGH = lax.Precision.HIGHEST

GELU_K = math.sqrt(2.0 / math.pi)
BETA = (GELU_K * 0.044715) ** (1.0 / 3.0)
KAPPA = GELU_K / BETA


def dot(a, b, dims=((1,), (0,)), precision=None):
    return lax.dot_general(
        a, b, (dims, ((), ())), preferred_element_type=F32, precision=precision
    )


def kernel(
    dims,
    state_hbm,
    memb_hbm,
    gain_hbm,
    wr_hbm,
    ws_hbm,
    wo_hbm,
    pairs_hbm,
    counts_ref,
    cot_hbm,
    new_ref,
    gst_ref,
    gr_ref,
    gs_ref,
    go_ref,
    state_ref,
    memb_ref,
    gain_ref,
    wr_ref,
    ws_ref,
    wo_ref,
    pairs_ref,
    cot_ref,
    x_buf,
    xs_buf,
    lists,
    win,
    proj,
    mask,
    pre_buf,
    dact_buf,
    a_buf,
    d_buf,
    pg_buf,
    msg_send,
    msg_recv,
    own_msg,
    sg_loc,
    sg_near,
    sg_reg,
    sg_peer,
    w_loc,
    w_send,
    w_recv,
    w_all,
    in_sem,
    list_ss,
    list_rs,
    win_ss,
    win_rs,
    msg_ss,
    msg_rs,
    near_ss,
    near_rs,
    peer_ss,
    peer_rs,
    red_ss,
    red_rs,
    gat_ss,
    gat_rs,
    fwd_ss,
    fwd_rs,
):
    nz, nh, ns = dims
    rows, width = state_ref.shape
    blocks = rows // BLK
    slots = pairs_ref.shape[1]
    quarter = wr_ref.shape[1]
    owners = nh * ns
    own_blocks = blocks // owners
    piece = own_blocks * BLK
    r = lax.axis_index("space")
    h = lax.axis_index("hidden")
    s = lax.axis_index("sub")
    after = lax.rem(r + 1, nz)
    before = lax.rem(r + nz - 1, nz)

    def peer(dh, ds):
        return lax.rem(h + dh, nh), lax.rem(s + ds, ns)

    offsets = [(dh, ds) for dh in range(nh - 1, -1, -1) for ds in range(ns - 1, -1, -1)]

    own_cols = pl.ds(pl.multiple_of(s * quarter, quarter), quarter)
    loads = [
        pltpu.make_async_copy(src, dst, in_sem.at[n])
        for n, (src, dst) in enumerate(
            (
                (memb_hbm, memb_ref),
                (state_hbm, state_ref),
                (gain_hbm, gain_ref),
                (pairs_hbm, pairs_ref),
                (wr_hbm.at[:, own_cols], wr_ref),
                (cot_hbm, cot_ref),
                (wo_hbm.at[own_cols, :], wo_ref),
                (ws_hbm.at[:, own_cols], ws_ref),
            )
        )
    ]
    for load in loads:
        load.start()

    barrier = pltpu.get_barrier_semaphore()
    met = 0
    for k in range(1, nz):
        pl.semaphore_signal(
            barrier, inc=1, device_id={"space": lax.rem(r + k, nz)}, device_id_type=MESH
        )
        met += 1
    for dh, ds in offsets[:-1]:
        ph, ps = peer(dh, ds)
        pl.semaphore_signal(
            barrier, inc=1, device_id={"hidden": ph, "sub": ps}, device_id_type=MESH
        )
        met += 1
    for ds in range(1, ns):
        for other in (after, before):
            pl.semaphore_signal(
                barrier,
                inc=1,
                device_id={"space": other, "sub": lax.rem(s + ds, ns)},
                device_id_type=MESH,
            )
            met += 1

    for load in loads[:4]:
        load.wait()

    live = lax.broadcasted_iota(jnp.int32, (slots, 128), 0) < counts_ref[0]
    diagonal = lax.broadcasted_iota(jnp.int32, (slots, slots), 0) == lax.broadcasted_iota(
        jnp.int32, (slots, slots), 1
    )
    for column in range(2):
        ids = jnp.where(diagonal, pairs_ref[column : column + 1, :].astype(F32), 0.0)
        ids = jnp.sum(ids, axis=1, keepdims=True).astype(jnp.int32)
        ids = jnp.broadcast_to(ids, (slots, 128))
        lists[0, column * slots : (column + 1) * slots, :] = jnp.where(live, ids, -1000000)

    gain = gain_ref[...]
    for k in range(rows // 256):
        hot = lax.broadcasted_iota(jnp.int32, (rows, 256), 0) == memb_ref[:, k * 256 : (k + 1) * 256]
        xs = dot(hot.astype(F32).astype(BF16), state_ref[...], ((0,), (0,)))
        factor = lax.rsqrt(jnp.mean(xs * xs, axis=-1, keepdims=True) + 1e-06)
        normed = (xs * factor * gain).astype(BF16)
        x_buf[k * 256 : (k + 1) * 256, :] = normed
        xs_buf[k * 256 : (k + 1) * 256, :] = xs.astype(BF16)
        means = jnp.sum(normed.astype(F32).reshape(256 // BLK, BLK, width), axis=1) / BLK
        first = blocks + k * (256 // BLK)
        win[first : first + 256 // BLK, :] = means.astype(BF16).astype(F32)

    pl.semaphore_wait(barrier, met)

    copies = []

    def send(src, dst, ss, rs, where):
        copy = pltpu.make_async_remote_copy(
            src_ref=src,
            dst_ref=dst,
            send_sem=ss,
            recv_sem=rs,
            device_id=where,
            device_id_type=MESH,
        )
        copy.start()
        return copy

    for n, (other, place) in enumerate(((before, 2 * blocks), (after, 0))):
        copies.append(
            send(
                win.at[pl.ds(blocks, blocks)],
                win.at[pl.ds(place, blocks)],
                win_ss.at[n],
                win_rs.at[n],
                {"space": other},
            )
        )
    for ds in range(1, ns):
        copies.append(
            send(
                lists.at[0],
                lists.at[ds],
                list_ss.at[ds - 1],
                list_rs.at[ds - 1],
                {"sub": lax.rem(s + ds, ns)},
            )
        )
    for ds in range(ns):
        copies.append(
            send(
                lists.at[0],
                lists.at[ns + ds],
                list_ss.at[ns - 1 + ds],
                list_rs.at[ns - 1 + ds],
                {"space": after, "sub": lax.rem(s + ds, ns)},
            )
        )

    for load in loads[4:]:
        load.wait()
    wr = wr_ref[...]
    wo = wo_ref[...]
    ws = ws_ref[...]
    for k in range(rows // 256):
        part = slice(k * 256, (k + 1) * 256)
        pre_buf[part, :] = dot(x_buf[part, :], wr) * BETA
        dact_buf[part, :] = dot(cot_ref[part, :], wo, ((1,), (1,)))
    pg_buf[...] = jnp.zeros_like(pg_buf)

    for copy in copies:
        copy.wait()

    span = 4 * blocks
    base = r * blocks
    marks = []
    lane = lax.broadcasted_iota(jnp.int32, (slots, 128), 1)
    for n in range(2 * ns):
        source = lists[n, 0:slots, :] - base
        target = lists[n, slots : 2 * slots, :] - base
        for recv, sender in ((target, source), (source, target)):
            inside = (recv >= 0) & (recv < blocks)
            place = jnp.where(inside, recv * span + (sender - recv + blocks), -1)
            marks.append(
                jnp.concatenate(
                    [
                        (place == lane + c * 128).astype(F32).astype(BF16)
                        for c in range(blocks * span // 128)
                    ],
                    axis=1,
                )
            )
    marks = jnp.concatenate(marks, axis=0)
    mask[...] = dot(marks, jnp.ones((marks.shape[0], quarter), BF16), ((0,), (0,)))
    proj[...] = dot(win[...].astype(BF16), ws) * BETA

    def one_block(a):
        def one_chunk(c, carry):
            here = pl.ds(pl.multiple_of(a * BLK + c * CHUNK, CHUNK), CHUNK)
            v0 = pre_buf[here, :]
            da = dact_buf[here, :]
            act_sum = jnp.zeros((CHUNK, quarter), F32)
            d_sum = jnp.zeros((CHUNK, quarter), F32)
            for d in range(2 * blocks + 1):
                if d == blocks:
                    continue
                v = v0 + proj[pl.ds(a + d, 1), :]
                v2 = v * v
                t = jnp.tanh(v * (v2 + KAPPA))
                rise = (1.0 + t) * mask[pl.ds(a * span + d, 1), :]
                act = v * rise
                act_sum = act_sum + act
                slope = rise + act * (1.0 - t) * (3.0 * v2 + KAPPA)
                d_pre = da * slope
                d_sum = d_sum + d_pre
                pg = pl.ds(pl.multiple_of((a + d) * 8, 8), 8)
                total = d_pre[0:8, :]
                for i in range(1, CHUNK // 8):
                    total = total + d_pre[i * 8 : (i + 1) * 8, :]
                pg_buf[pg, :] = pg_buf[pg, :] + total
            a_buf[here, :] = (act_sum * (0.5 / BETA)).astype(BF16)
            d_buf[here, :] = (d_sum * 0.5).astype(BF16)
            return carry

        lax.fori_loop(0, BLK // CHUNK, one_chunk, 0)

    msg_copies = []
    for n, (dh, ds) in enumerate(offsets):
        ph, ps = peer(dh, ds)
        first = (ph * ns + ps) * own_blocks

        def step(i, carry, first=first):
            one_block(first + i)
            return carry

        lax.fori_loop(0, own_blocks, step, 0)
        here = pl.ds(pl.multiple_of(first * BLK, BLK), piece)
        message = dot(a_buf[here, :], wo)
        grads = dot(d_buf[here, :], wr, ((1,), (1,)))
        if n < owners - 1:
            msg_send[n, 0:piece, :] = message.astype(BF16)
            msg_send[n, piece : 2 * piece, :] = grads.astype(BF16)
            msg_copies.append(
                send(
                    msg_send.at[n],
                    msg_recv.at[n],
                    msg_ss.at[n],
                    msg_rs.at[n],
                    {"hidden": ph, "sub": ps},
                )
            )
        else:
            own_msg[0:piece, :] = message
            own_msg[piece : 2 * piece, :] = grads

    pg = jnp.sum(pg_buf[...].reshape(3 * blocks, 8, quarter), axis=1) * 0.5
    sg_loc[...] = dot(pg, ws.astype(F32), ((1,), (1,)), HIGH)
    near = [
        send(
            sg_loc.at[pl.ds(place, blocks)],
            sg_near.at[n],
            near_ss.at[n],
            near_rs.at[n],
            {"space": other},
        )
        for n, (other, place) in enumerate(((before, 0), (after, 2 * blocks)))
    ]

    w_loc[0:width, :] = dot(x_buf[...], d_buf[...], ((0,), (0,)))
    w_loc[width : 2 * width, :] = dot(win[...], pg, ((0,), (0,)), HIGH)
    for c in range(width // quarter):
        w_loc[2 * width + c * quarter : 2 * width + (c + 1) * quarter, :] = dot(
            a_buf[...], cot_ref[:, c * quarter : (c + 1) * quarter], ((0,), (0,))
        )
    travel = w_send.dtype
    w_send[...] = w_loc[...].astype(travel)
    share = 3 * width // nz

    def share_at(index):
        return pl.ds(pl.multiple_of(index * share, share), share)

    reduces = []
    for k in range(1, nz):
        to = lax.rem(r + k, nz)
        reduces.append(
            send(
                w_send.at[share_at(to)],
                w_recv.at[k - 1],
                red_ss.at[k - 1],
                red_rs.at[k - 1],
                {"space": to},
            )
        )

    for copy in near:
        copy.wait()
    sg_reg[...] = sg_loc[blocks : 2 * blocks, :] + sg_near[0] + sg_near[1]
    peers = []
    for n, (dh, ds) in enumerate(offsets[:-1]):
        ph, ps = peer(dh, ds)
        peers.append(
            send(
                sg_reg,
                sg_peer.at[n],
                peer_ss.at[n],
                peer_rs.at[n],
                {"hidden": ph, "sub": ps},
            )
        )

    for copy in reduces:
        copy.wait_recv()
    total = w_loc[share_at(r), :]
    for k in range(1, nz):
        total = total + w_recv[k - 1].astype(F32)
    w_all[0, share_at(r), :] = total.astype(travel)
    gathers = []
    forwards = []
    for k in range(1, nz):
        gathers.append(
            send(
                w_all.at[0, share_at(r)],
                w_all.at[0, share_at(r)],
                gat_ss.at[k - 1],
                gat_rs.at[k - 1],
                {"space": lax.rem(r + k, nz)},
            )
        )

    def forward(k):
        origin = share_at(lax.rem(r + nz - k, nz))
        for ds in range(1, ns):
            forwards.append(
                send(
                    w_all.at[0, origin],
                    w_all.at[ds, origin],
                    fwd_ss.at[ds - 1, k],
                    fwd_rs.at[ds - 1, k],
                    {"sub": lax.rem(s + ds, ns)},
                )
            )

    forward(0)

    for copy in msg_copies:
        copy.wait()
    for copy in peers:
        copy.wait()
    message = own_msg[0:piece, :]
    grads = own_msg[piece : 2 * piece, :]
    near_sum = sg_reg[...]
    for n in range(owners - 1):
        message = message + msg_recv[n, 0:piece, :].astype(F32)
        grads = grads + msg_recv[n, piece : 2 * piece, :].astype(F32)
        near_sum = near_sum + sg_peer[n]
    sg_loc[0:blocks, :] = near_sum / BLK
    q = h * ns + s
    mine = pl.ds(pl.multiple_of(q * piece, piece), piece)
    xs = xs_buf[mine, :].astype(F32)
    new_ref[...] = (xs + message).astype(BF16)
    spread = jnp.concatenate(
        [
            jnp.broadcast_to(sg_loc[pl.ds(q * own_blocks + i, 1), :], (BLK, width))
            for i in range(own_blocks)
        ],
        axis=0,
    )
    factor = lax.rsqrt(jnp.mean(xs * xs, axis=-1, keepdims=True) + 1e-06)
    scaled = (grads + spread) * gain
    inner = jnp.mean(xs * scaled, axis=-1, keepdims=True)
    gst_ref[...] = (
        factor * scaled - xs * factor * factor * factor * inner + cot_ref[mine, :].astype(F32)
    )

    for k in range(1, nz):
        gathers[k - 1].wait_recv()
        forward(k)
    for copy in forwards:
        copy.wait_recv()
    for ds in range(ns):
        begin = pl.multiple_of(lax.rem(s + ns - ds, ns) * quarter, quarter)
        cols = pl.ds(begin, quarter)
        gr_ref[:, cols] = w_all[ds, 0:width, :].astype(F32)
        gs_ref[:, cols] = w_all[ds, width : 2 * width, :].astype(F32)
        for c in range(width // quarter):
            at = 2 * width + c * quarter
            go_ref[cols, c * quarter : (c + 1) * quarter] = w_all[ds, at : at + quarter, :].astype(
                F32
            )
    for copy in reduces + gathers + forwards:
        copy.wait_send()


def store(new_in, gst_in, gr_in, gs_in, go_in, new_out, gst_out, gr_out, gs_out, go_out, sem):
    copies = [
        pltpu.make_async_copy(src, dst, sem.at[n])
        for n, (src, dst) in enumerate(
            (
                (gr_in, gr_out),
                (gs_in, gs_out),
                (go_in, go_out),
                (gst_in, gst_out),
                (new_in, new_out),
            )
        )
    ]
    for copy in copies:
        copy.start()
    for copy in copies:
        copy.wait()


def on_device(
    dims,
    agent_state,
    members,
    norm_gain,
    w_recv,
    w_send,
    w_out,
    pair_list,
    pair_counts,
    cotangent,
):
    nz, nh, ns = dims
    rows, width = agent_state.shape
    blocks = rows // BLK
    slots = pair_list.shape[0]
    hid_dev = w_recv.shape[1]
    quarter = hid_dev // ns
    owners = nh * ns
    piece = rows // owners
    share = 3 * width // nz
    travel = BF16 if share % 16 == 0 else F32
    dma = pltpu.SemaphoreType.DMA
    vmem = pl.BlockSpec(memory_space=pltpu.VMEM)
    smem = pl.BlockSpec(memory_space=pltpu.SMEM)
    hbm = pl.BlockSpec(memory_space=pltpu.HBM)
    out_shape = (
        jax.ShapeDtypeStruct((piece, width), BF16),
        jax.ShapeDtypeStruct((piece, width), F32),
        jax.ShapeDtypeStruct((width, hid_dev), F32),
        jax.ShapeDtypeStruct((width, hid_dev), F32),
        jax.ShapeDtypeStruct((hid_dev, width), F32),
    )
    results = pl.pallas_call(
        functools.partial(kernel, dims),
        out_shape=out_shape,
        in_specs=[hbm] * 7 + [smem, hbm],
        out_specs=(vmem,) * 5,
        scratch_shapes=[
            pltpu.VMEM((rows, width), BF16),
            pltpu.VMEM((1, rows), jnp.int32),
            pltpu.VMEM((1, width), F32),
            pltpu.VMEM((width, quarter), BF16),
            pltpu.VMEM((width, quarter), BF16),
            pltpu.VMEM((quarter, width), BF16),
            pltpu.VMEM((2, slots), jnp.int32),
            pltpu.VMEM((rows, width), BF16),
            pltpu.VMEM((rows, width), BF16),
            pltpu.VMEM((rows, width), BF16),
            pltpu.VMEM((2 * ns, 2 * slots, 128), jnp.int32),
            pltpu.VMEM((3 * blocks, width), F32),
            pltpu.VMEM((3 * blocks, quarter), F32),
            pltpu.VMEM((4 * blocks * blocks, quarter), F32),
            pltpu.VMEM((rows, quarter), F32),
            pltpu.VMEM((rows, quarter), F32),
            pltpu.VMEM((rows, quarter), BF16),
            pltpu.VMEM((rows, quarter), BF16),
            pltpu.VMEM((3 * blocks * 8, quarter), F32),
            pltpu.VMEM((owners - 1, 2 * piece, width), BF16),
            pltpu.VMEM((owners - 1, 2 * piece, width), BF16),
            pltpu.VMEM((2 * piece, width), F32),
            pltpu.VMEM((3 * blocks, width), F32),
            pltpu.VMEM((2, blocks, width), F32),
            pltpu.VMEM((blocks, width), F32),
            pltpu.VMEM((owners - 1, blocks, width), F32),
            pltpu.VMEM((3 * width, quarter), F32),
            pltpu.VMEM((3 * width, quarter), travel),
            pltpu.VMEM((nz - 1, share, quarter), travel),
            pltpu.VMEM((ns, 3 * width, quarter), travel),
            dma((8,)),
            dma((2 * ns - 1,)),
            dma((2 * ns - 1,)),
            dma((2,)),
            dma((2,)),
            dma((owners - 1,)),
            dma((owners - 1,)),
            dma((2,)),
            dma((2,)),
            dma((owners - 1,)),
            dma((owners - 1,)),
            dma((nz - 1,)),
            dma((nz - 1,)),
            dma((nz - 1,)),
            dma((nz - 1,)),
            dma((ns - 1, nz)),
            dma((ns - 1, nz)),
        ],
        compiler_params=pltpu.CompilerParams(
            collective_id=0, has_side_effects=True, vmem_limit_bytes=64 * 1024 * 1024
        ),
    )(
        agent_state,
        members,
        norm_gain.reshape(1, width),
        w_recv,
        w_send,
        w_out,
        pair_list.T,
        pair_counts,
        cotangent,
    )
    return pl.pallas_call(
        store,
        out_shape=out_shape,
        in_specs=[hbm] * 5,
        out_specs=(hbm,) * 5,
        scratch_shapes=[dma((5,))],
        compiler_params=pltpu.CompilerParams(vmem_limit_bytes=64 * 1024 * 1024),
    )(*results)


def solution(mesh):
    in_specs = (
        P(("groups", "space"), None),
        P(("groups", "space"), None),
        P(),
        P(None, "hidden"),
        P(None, "hidden"),
        P("hidden", None),
        P(("groups", "space", "sub"), None),
        P(("groups", "space", "sub")),
        P(("groups", "space"), None),
    )
    out_specs = (
        P(("groups", "space", "hidden", "sub"), None),
        P(("groups", "space", "hidden", "sub"), None),
        P("groups", "hidden"),
        P("groups", "hidden"),
        P(("groups", "hidden"), None),
    )
    dims = (mesh.shape["space"], mesh.shape["hidden"], mesh.shape["sub"])
    return jax.shard_map(
        functools.partial(on_device, dims),
        mesh=mesh,
        in_specs=in_specs,
        out_specs=out_specs,
        check_vma=False,
    )
```

```python
import functools
import math

import jax
import jax.numpy as jnp
from jax import lax
from jax.experimental import pallas as pl
from jax.experimental.pallas import tpu as pltpu
from jax.sharding import PartitionSpec as P

BLK = 128
CHUNK = 32
LANES = 128
BF16 = jnp.bfloat16
F32 = jnp.float32
MESH = pl.DeviceIdType.MESH
HIGH = lax.Precision.HIGHEST

GELU_K = math.sqrt(2.0 / math.pi)
BETA = (GELU_K * 0.044715) ** (1.0 / 3.0)
KAPPA = GELU_K / BETA


def dot(a, b, dims=((1,), (0,)), precision=None):
    return lax.dot_general(
        a, b, (dims, ((), ())), preferred_element_type=F32, precision=precision
    )


def kernel(
    dims,
    state_hbm,
    memb_hbm,
    gain_hbm,
    wr_hbm,
    ws_hbm,
    wo_hbm,
    pairs_hbm,
    counts_ref,
    cot_hbm,
    new_ref,
    gst_ref,
    gr_ref,
    gs_ref,
    go_ref,
    state_ref,
    memb_ref,
    gain_ref,
    wr_ref,
    ws_ref,
    wo_ref,
    pairs_ref,
    cot_ref,
    x_buf,
    xs_buf,
    lists,
    win,
    proj,
    mask,
    pre_buf,
    dact_buf,
    a_buf,
    d_buf,
    pg_buf,
    msg_send,
    msg_recv,
    own_msg,
    sg_loc,
    sg_near,
    sg_reg,
    sg_peer,
    w_loc,
    w_send,
    w_recv,
    w_all,
    in_sem,
    list_ss,
    list_rs,
    win_ss,
    win_rs,
    msg_ss,
    msg_rs,
    near_ss,
    near_rs,
    peer_ss,
    peer_rs,
    red_ss,
    red_rs,
    gat_ss,
    gat_rs,
    fwd_ss,
    fwd_rs,
):
    nz, nh, ns = dims
    rows, width = state_ref.shape
    blocks = rows // BLK
    slots = pairs_ref.shape[1]
    quarter = wr_ref.shape[1]
    owners = nh * ns
    own_blocks = blocks // owners
    piece = own_blocks * BLK
    r = lax.axis_index("space")
    h = lax.axis_index("hidden")
    s = lax.axis_index("sub")
    after = lax.rem(r + 1, nz)
    before = lax.rem(r + nz - 1, nz)

    def peer(dh, ds):
        return lax.rem(h + dh, nh), lax.rem(s + ds, ns)

    offsets = [(dh, ds) for dh in range(nh - 1, -1, -1) for ds in range(ns - 1, -1, -1)]

    own_cols = pl.ds(pl.multiple_of(s * quarter, quarter), quarter)
    loads = [
        pltpu.make_async_copy(src, dst, in_sem.at[n])
        for n, (src, dst) in enumerate(
            (
                (memb_hbm, memb_ref),
                (state_hbm, state_ref),
                (gain_hbm, gain_ref),
                (pairs_hbm, pairs_ref),
                (wr_hbm.at[:, own_cols], wr_ref),
                (cot_hbm, cot_ref),
                (wo_hbm.at[own_cols, :], wo_ref),
                (ws_hbm.at[:, own_cols], ws_ref),
            )
        )
    ]
    for load in loads:
        load.start()

    barrier = pltpu.get_barrier_semaphore()
    met = 0
    for k in range(1, nz):
        pl.semaphore_signal(
            barrier, inc=1, device_id={"space": lax.rem(r + k, nz)}, device_id_type=MESH
        )
        met += 1
    for dh, ds in offsets[:-1]:
        ph, ps = peer(dh, ds)
        pl.semaphore_signal(
            barrier, inc=1, device_id={"hidden": ph, "sub": ps}, device_id_type=MESH
        )
        met += 1
    for ds in range(1, ns):
        for other in (after, before):
            pl.semaphore_signal(
                barrier,
                inc=1,
                device_id={"space": other, "sub": lax.rem(s + ds, ns)},
                device_id_type=MESH,
            )
            met += 1

    for load in loads[:4]:
        load.wait()

    live = lax.broadcasted_iota(jnp.int32, (slots, 128), 0) < counts_ref[0]
    diagonal = lax.broadcasted_iota(jnp.int32, (slots, slots), 0) == lax.broadcasted_iota(
        jnp.int32, (slots, slots), 1
    )
    for column in range(2):
        ids = jnp.where(diagonal, pairs_ref[column : column + 1, :].astype(F32), 0.0)
        ids = jnp.sum(ids, axis=1, keepdims=True).astype(jnp.int32)
        ids = jnp.broadcast_to(ids, (slots, 128))
        lists[0, column * slots : (column + 1) * slots, :] = jnp.where(live, ids, -1000000)

    gain = gain_ref[...]
    for k in range(rows // 256):
        hot = lax.broadcasted_iota(jnp.int32, (rows, 256), 0) == memb_ref[:, k * 256 : (k + 1) * 256]
        xs = dot(hot.astype(F32).astype(BF16), state_ref[...], ((0,), (0,)))
        factor = lax.rsqrt(jnp.mean(xs * xs, axis=-1, keepdims=True) + 1e-06)
        normed = (xs * factor * gain).astype(BF16)
        x_buf[k * 256 : (k + 1) * 256, :] = normed
        xs_buf[k * 256 : (k + 1) * 256, :] = xs.astype(BF16)
        means = jnp.sum(normed.astype(F32).reshape(256 // BLK, BLK, width), axis=1) / BLK
        first = blocks + k * (256 // BLK)
        win[first : first + 256 // BLK, :] = means.astype(BF16).astype(F32)

    pl.semaphore_wait(barrier, met)

    copies = []

    def send(src, dst, ss, rs, where):
        copy = pltpu.make_async_remote_copy(
            src_ref=src,
            dst_ref=dst,
            send_sem=ss,
            recv_sem=rs,
            device_id=where,
            device_id_type=MESH,
        )
        copy.start()
        return copy

    for n, (other, place) in enumerate(((before, 2 * blocks), (after, 0))):
        copies.append(
            send(
                win.at[pl.ds(blocks, blocks)],
                win.at[pl.ds(place, blocks)],
                win_ss.at[n],
                win_rs.at[n],
                {"space": other},
            )
        )
    for ds in range(1, ns):
        copies.append(
            send(
                lists.at[0],
                lists.at[ds],
                list_ss.at[ds - 1],
                list_rs.at[ds - 1],
                {"sub": lax.rem(s + ds, ns)},
            )
        )
    for ds in range(ns):
        copies.append(
            send(
                lists.at[0],
                lists.at[ns + ds],
                list_ss.at[ns - 1 + ds],
                list_rs.at[ns - 1 + ds],
                {"space": after, "sub": lax.rem(s + ds, ns)},
            )
        )

    for load in loads[4:]:
        load.wait()
    wr = wr_ref[...]
    wo = wo_ref[...]
    ws = ws_ref[...]
    for k in range(rows // 256):
        part = slice(k * 256, (k + 1) * 256)
        pre_buf[part, :] = dot(x_buf[part, :], wr) * BETA
        dact_buf[part, :] = dot(cot_ref[part, :], wo, ((1,), (1,)))
    pg_buf[...] = jnp.zeros_like(pg_buf)

    for copy in copies:
        copy.wait()

    span = 4 * blocks
    base = r * blocks
    marks = []
    lane = lax.broadcasted_iota(jnp.int32, (slots, 128), 1)
    for n in range(2 * ns):
        source = lists[n, 0:slots, :] - base
        target = lists[n, slots : 2 * slots, :] - base
        for recv, sender in ((target, source), (source, target)):
            inside = (recv >= 0) & (recv < blocks)
            place = jnp.where(inside, recv * span + (sender - recv + blocks), -1)
            marks.append(
                jnp.concatenate(
                    [
                        (place == lane + c * 128).astype(F32).astype(BF16)
                        for c in range(blocks * span // 128)
                    ],
                    axis=1,
                )
            )
    marks = jnp.concatenate(marks, axis=0)
    mask[...] = dot(marks, jnp.ones((marks.shape[0], LANES), BF16), ((0,), (0,)))
    passes = quarter // LANES
    for p in range(passes):
        proj[p, :, :] = dot(win[...].astype(BF16), ws_ref[:, p * LANES : (p + 1) * LANES]) * BETA

    def one_block(a, p, cols):
        def one_chunk(c, carry):
            here = pl.ds(pl.multiple_of(a * BLK + c * CHUNK, CHUNK), CHUNK)
            v0 = pre_buf[here, cols]
            da = dact_buf[here, cols]
            act_sum = jnp.zeros((CHUNK, LANES), F32)
            d_sum = jnp.zeros((CHUNK, LANES), F32)
            for d in range(2 * blocks + 1):
                if d == blocks:
                    continue
                v = v0 + proj[p, pl.ds(a + d, 1), :]
                v2 = v * v
                t = jnp.tanh(v * (v2 + KAPPA))
                rise = (1.0 + t) * mask[pl.ds(a * span + d, 1), :]
                act = v * rise
                act_sum = act_sum + act
                slope = rise + act * (1.0 - t) * (3.0 * v2 + KAPPA)
                d_pre = da * slope
                d_sum = d_sum + d_pre
                pg = pl.ds(pl.multiple_of((a + d) * 8, 8), 8)
                total = d_pre[0:8, :]
                for i in range(1, CHUNK // 8):
                    total = total + d_pre[i * 8 : (i + 1) * 8, :]
                pg_buf[pg, cols] = pg_buf[pg, cols] + total
            a_buf[here, cols] = (act_sum * (0.5 / BETA)).astype(BF16)
            d_buf[here, cols] = (d_sum * 0.5).astype(BF16)
            return carry

        lax.fori_loop(0, BLK // CHUNK, one_chunk, 0)

    travel = w_send.dtype
    share = 3 * width // nz

    def share_at(index):
        return pl.ds(pl.multiple_of(index * share, share), share)

    def start_reduce(p, cols):
        pg = jnp.sum(pg_buf[:, cols].reshape(3 * blocks, 8, LANES), axis=1) * 0.5
        w_loc[p, 0:width, :] = dot(x_buf[...], d_buf[:, cols], ((0,), (0,)))
        w_loc[p, width : 2 * width, :] = dot(win[...], pg, ((0,), (0,)), HIGH)
        outer = dot(a_buf[:, cols], cot_ref[...], ((0,), (0,)))
        for c in range(width // LANES):
            w_loc[p, 2 * width + c * LANES : 2 * width + (c + 1) * LANES, :] = outer[
                :, c * LANES : (c + 1) * LANES
            ]
        w_send[p, :, :] = w_loc[p].astype(travel)
        started = []
        for k in range(1, nz):
            to = lax.rem(r + k, nz)
            started.append(
                send(
                    w_send.at[p, share_at(to)],
                    w_recv.at[p, k - 1],
                    red_ss.at[p, k - 1],
                    red_rs.at[p, k - 1],
                    {"space": to},
                )
            )
        return started

    def forward(p, k):
        origin = share_at(lax.rem(r + nz - k, nz))
        return [
            send(
                w_all.at[0, p, origin],
                w_all.at[ds, p, origin],
                fwd_ss.at[p, ds - 1, k],
                fwd_rs.at[p, ds - 1, k],
                {"sub": lax.rem(s + ds, ns)},
            )
            for ds in range(1, ns)
        ]

    def start_gather(p, started):
        for copy in started:
            copy.wait_recv()
        total = w_loc[p, share_at(r), :]
        for k in range(1, nz):
            total = total + w_recv[p, k - 1].astype(F32)
        w_all[0, p, share_at(r), :] = total.astype(travel)
        gathered = [
            send(
                w_all.at[0, p, share_at(r)],
                w_all.at[0, p, share_at(r)],
                gat_ss.at[p, k - 1],
                gat_rs.at[p, k - 1],
                {"space": lax.rem(r + k, nz)},
            )
            for k in range(1, nz)
        ]
        return gathered, forward(p, 0)

    def finish_gather(p, gathered):
        passed = []
        for k in range(1, nz):
            gathered[k - 1].wait_recv()
            passed += forward(p, k)
        return passed

    def write_out(p, ds):
        begin = pl.multiple_of(lax.rem(s + ns - ds, ns) * quarter + p * LANES, LANES)
        at = pl.ds(begin, LANES)
        gr_ref[:, at] = w_all[ds, p, 0:width, :].astype(F32)
        gs_ref[:, at] = w_all[ds, p, width : 2 * width, :].astype(F32)
        for c in range(width // LANES):
            rows_c = slice(2 * width + c * LANES, 2 * width + (c + 1) * LANES)
            go_ref[at, c * LANES : (c + 1) * LANES] = w_all[ds, p, rows_c, :].astype(F32)

    msg_copies = []
    reduces = []
    gathers = []
    forwards = []
    for p in range(passes):
        cols = slice(p * LANES, (p + 1) * LANES)
        for n, (dh, ds) in enumerate(offsets):
            ph, ps = peer(dh, ds)
            first = (ph * ns + ps) * own_blocks

            def step(i, carry, first=first, p=p, cols=cols):
                one_block(first + i, p, cols)
                return carry

            lax.fori_loop(0, own_blocks, step, 0)
            if p > 0 and n == owners // 2:
                gathered, passed = start_gather(p - 1, reduces[p - 1])
                gathers.append(gathered)
                forwards.append(passed)
            if p < passes - 1:
                continue
            here = pl.ds(pl.multiple_of(first * BLK, BLK), piece)
            message = dot(a_buf[here, :], wo)
            grads = dot(d_buf[here, :], wr, ((1,), (1,)))
            if n < owners - 1:
                msg_send[n, 0:piece, :] = message.astype(BF16)
                msg_send[n, piece : 2 * piece, :] = grads.astype(BF16)
                msg_copies.append(
                    send(
                        msg_send.at[n],
                        msg_recv.at[n],
                        msg_ss.at[n],
                        msg_rs.at[n],
                        {"hidden": ph, "sub": ps},
                    )
                )
            else:
                own_msg[0:piece, :] = message
                own_msg[piece : 2 * piece, :] = grads
        reduces.append(start_reduce(p, cols))

    pg = jnp.sum(pg_buf[...].reshape(3 * blocks, 8, quarter), axis=1) * 0.5
    sg_loc[...] = dot(pg, ws.astype(F32), ((1,), (1,)), HIGH)
    near = [
        send(
            sg_loc.at[pl.ds(place, blocks)],
            sg_near.at[n],
            near_ss.at[n],
            near_rs.at[n],
            {"space": other},
        )
        for n, (other, place) in enumerate(((before, 0), (after, 2 * blocks)))
    ]
    for p in range(passes - 1):
        forwards[p] += finish_gather(p, gathers[p])

    for copy in near:
        copy.wait()
    sg_reg[...] = sg_loc[blocks : 2 * blocks, :] + sg_near[0] + sg_near[1]
    peers = []
    for n, (dh, ds) in enumerate(offsets[:-1]):
        ph, ps = peer(dh, ds)
        peers.append(
            send(
                sg_reg,
                sg_peer.at[n],
                peer_ss.at[n],
                peer_rs.at[n],
                {"hidden": ph, "sub": ps},
            )
        )
    for p in range(passes - 1):
        write_out(p, 0)

    gathered, passed = start_gather(passes - 1, reduces[passes - 1])
    gathers.append(gathered)
    forwards.append(passed)

    for copy in msg_copies:
        copy.wait()
    for copy in peers:
        copy.wait()
    message = own_msg[0:piece, :]
    grads = own_msg[piece : 2 * piece, :]
    near_sum = sg_reg[...]
    for n in range(owners - 1):
        message = message + msg_recv[n, 0:piece, :].astype(F32)
        grads = grads + msg_recv[n, piece : 2 * piece, :].astype(F32)
        near_sum = near_sum + sg_peer[n]
    sg_loc[0:blocks, :] = near_sum / BLK
    q = h * ns + s
    mine = pl.ds(pl.multiple_of(q * piece, piece), piece)
    xs = xs_buf[mine, :].astype(F32)
    new_ref[...] = (xs + message).astype(BF16)
    spread = jnp.concatenate(
        [
            jnp.broadcast_to(sg_loc[pl.ds(q * own_blocks + i, 1), :], (BLK, width))
            for i in range(own_blocks)
        ],
        axis=0,
    )
    factor = lax.rsqrt(jnp.mean(xs * xs, axis=-1, keepdims=True) + 1e-06)
    scaled = (grads + spread) * gain
    inner = jnp.mean(xs * scaled, axis=-1, keepdims=True)
    gst_ref[...] = (
        factor * scaled - xs * factor * factor * factor * inner + cot_ref[mine, :].astype(F32)
    )

    for p in range(passes - 1):
        for copy in forwards[p]:
            copy.wait_recv()
        for ds in range(1, ns):
            write_out(p, ds)
    last = passes - 1
    forwards[last] += finish_gather(last, gathers[last])
    write_out(last, 0)
    for copy in forwards[last]:
        copy.wait_recv()
    for ds in range(1, ns):
        write_out(last, ds)
    for p in range(passes):
        for copy in reduces[p] + gathers[p] + forwards[p]:
            copy.wait_send()


def store(*refs):
    ins, outs, held, (sem,) = refs[:5], refs[5:10], refs[10:15], refs[15:]
    loads = [pltpu.make_async_copy(ins[n], held[n], sem.at[0, n]) for n in range(5)]
    for load in loads:
        load.start()
    stores = []
    for n in (0, 1, 2, 3, 4):
        loads[n].wait()
        stores.append(pltpu.make_async_copy(held[n], outs[n], sem.at[1, n]))
        stores[-1].start()
    for copy in stores:
        copy.wait()


def on_device(
    dims,
    agent_state,
    members,
    norm_gain,
    w_recv,
    w_send,
    w_out,
    pair_list,
    pair_counts,
    cotangent,
):
    nz, nh, ns = dims
    rows, width = agent_state.shape
    blocks = rows // BLK
    slots = pair_list.shape[0]
    hid_dev = w_recv.shape[1]
    quarter = hid_dev // ns
    owners = nh * ns
    piece = rows // owners
    passes = quarter // LANES
    share = 3 * width // nz
    travel = BF16 if share % 16 == 0 else F32
    dma = pltpu.SemaphoreType.DMA
    vmem = pl.BlockSpec(memory_space=pltpu.VMEM)
    smem = pl.BlockSpec(memory_space=pltpu.SMEM)
    hbm = pl.BlockSpec(memory_space=pltpu.HBM)
    out_shape = (
        jax.ShapeDtypeStruct((piece, width), BF16),
        jax.ShapeDtypeStruct((piece, width), F32),
        jax.ShapeDtypeStruct((width, hid_dev), F32),
        jax.ShapeDtypeStruct((width, hid_dev), F32),
        jax.ShapeDtypeStruct((hid_dev, width), F32),
    )
    results = pl.pallas_call(
        functools.partial(kernel, dims),
        out_shape=out_shape,
        in_specs=[hbm] * 7 + [smem, hbm],
        out_specs=(vmem,) * 5,
        scratch_shapes=[
            pltpu.VMEM((rows, width), BF16),
            pltpu.VMEM((1, rows), jnp.int32),
            pltpu.VMEM((1, width), F32),
            pltpu.VMEM((width, quarter), BF16),
            pltpu.VMEM((width, quarter), BF16),
            pltpu.VMEM((quarter, width), BF16),
            pltpu.VMEM((2, slots), jnp.int32),
            pltpu.VMEM((rows, width), BF16),
            pltpu.VMEM((rows, width), BF16),
            pltpu.VMEM((rows, width), BF16),
            pltpu.VMEM((2 * ns, 2 * slots, 128), jnp.int32),
            pltpu.VMEM((3 * blocks, width), F32),
            pltpu.VMEM((passes, 3 * blocks, LANES), F32),
            pltpu.VMEM((4 * blocks * blocks, LANES), F32),
            pltpu.VMEM((rows, quarter), F32),
            pltpu.VMEM((rows, quarter), F32),
            pltpu.VMEM((rows, quarter), BF16),
            pltpu.VMEM((rows, quarter), BF16),
            pltpu.VMEM((3 * blocks * 8, quarter), F32),
            pltpu.VMEM((owners - 1, 2 * piece, width), BF16),
            pltpu.VMEM((owners - 1, 2 * piece, width), BF16),
            pltpu.VMEM((2 * piece, width), F32),
            pltpu.VMEM((3 * blocks, width), F32),
            pltpu.VMEM((2, blocks, width), F32),
            pltpu.VMEM((blocks, width), F32),
            pltpu.VMEM((owners - 1, blocks, width), F32),
            pltpu.VMEM((passes, 3 * width, LANES), F32),
            pltpu.VMEM((passes, 3 * width, LANES), travel),
            pltpu.VMEM((passes, nz - 1, share, LANES), travel),
            pltpu.VMEM((ns, passes, 3 * width, LANES), travel),
            dma((8,)),
            dma((2 * ns - 1,)),
            dma((2 * ns - 1,)),
            dma((2,)),
            dma((2,)),
            dma((owners - 1,)),
            dma((owners - 1,)),
            dma((2,)),
            dma((2,)),
            dma((owners - 1,)),
            dma((owners - 1,)),
            dma((passes, nz - 1)),
            dma((passes, nz - 1)),
            dma((passes, nz - 1)),
            dma((passes, nz - 1)),
            dma((passes, ns - 1, nz)),
            dma((passes, ns - 1, nz)),
        ],
        compiler_params=pltpu.CompilerParams(
            collective_id=0, has_side_effects=True, vmem_limit_bytes=64 * 1024 * 1024
        ),
    )(
        agent_state,
        members,
        norm_gain.reshape(1, width),
        w_recv,
        w_send,
        w_out,
        pair_list.T,
        pair_counts,
        cotangent,
    )
    return pl.pallas_call(
        store,
        out_shape=out_shape,
        in_specs=[hbm] * 5,
        out_specs=(hbm,) * 5,
        scratch_shapes=[pltpu.VMEM(one.shape, one.dtype) for one in out_shape] + [dma((2, 5))],
        compiler_params=pltpu.CompilerParams(vmem_limit_bytes=64 * 1024 * 1024),
    )(*results)


def solution(mesh):
    in_specs = (
        P(("groups", "space"), None),
        P(("groups", "space"), None),
        P(),
        P(None, "hidden"),
        P(None, "hidden"),
        P("hidden", None),
        P(("groups", "space", "sub"), None),
        P(("groups", "space", "sub")),
        P(("groups", "space"), None),
    )
    out_specs = (
        P(("groups", "space", "hidden", "sub"), None),
        P(("groups", "space", "hidden", "sub"), None),
        P("groups", "hidden"),
        P("groups", "hidden"),
        P(("groups", "hidden"), None),
    )
    dims = (mesh.shape["space"], mesh.shape["hidden"], mesh.shape["sub"])
    return jax.shard_map(
        functools.partial(on_device, dims),
        mesh=mesh,
        in_specs=in_specs,
        out_specs=out_specs,
        check_vma=False,
    )
```
